512 devices in a mesh: req: 32 (over z_lo, x), seq: 16 (over y, z_hi, core).
Axes of the slice: x: 4, y: 4, z: 16 (z_hi: 2, z_lo: 8; z = z_hi * 8 + z_lo), core: 2. Of those that a mesh axis runs over, the one named last changes fastest.
Arguments:
- query_block: bfloat16 [32, 16, 64, 10240], P('req', 'seq'), may hold values from -40 to 40
- k_cache: bfloat16 [32, 10752, 1024], P('req', 'seq'), may hold values from -40 to 40
- v_cache: bfloat16 [32, 10752, 1024], P('req', 'seq'), may hold values from -6 to 6
- ctx_len: int32 [32], P('req'), may hold values from 5376 to 10752, as said below
- host: int32 [32], P('req'), may hold values from 0 to 15
Outputs:
- attended: bfloat16 [32, 16, 64, 8192], P('req', 'seq')
The draws below stay inside these ranges and needn't reach their ends.
Inputs may be any that keep to these rules, and one draw needn't show every extreme that they name: ctx_len lies between 5376 and 10752; the largest equals 10752.
All inputs are finite; a program needn't handle non-finite values.
Results may differ from the reference program's by a relative error of at most 0.0046.
Values may be sent and summed in bfloat16 or wider, within the bound.
A program may use at most 128 MiB of HBM per device.

```python
import math
import jax
import jax.numpy as jnp
from jax import lax

HQ = 64
HK = 8
DH = 128
Q = 64
CTX_DEV = 672
CONTEXT = 10752
REQUESTS = 32
N_SEQ = 16


def draw_query_block(key, part):
    key = jax.random.fold_in(key, 11)
    shape = (REQUESTS, N_SEQ, Q, (HQ + 2 * HK) * DH)
    base = jnp.clip(jax.random.normal(key, shape, jnp.float32), -6.0, 6.0)
    return base.astype(jnp.bfloat16)


def draw_k_cache(key, part):
    key = jax.random.fold_in(key, 13)
    shape = (REQUESTS, CONTEXT, HK * DH)
    base = jnp.clip(jax.random.normal(key, shape, jnp.float32), -6.0, 6.0)
    return base.astype(jnp.bfloat16)


def draw_ctx_len(key, part):
    key = jax.random.fold_in(key, 17)
    length_key = jax.random.fold_in(key, 1)
    where_key = jax.random.fold_in(key, 2)
    lengths = jax.random.randint(length_key, (REQUESTS,), CONTEXT // 2, CONTEXT + 1, jnp.int32)
    longest = jax.random.randint(where_key, (), 0, REQUESTS, jnp.int32)
    return lengths.at[longest].set(CONTEXT)


def set_ends(entries, key, smallest, top_value):
    longest = entries.shape.index(max(entries.shape))
    spots = []
    for shift in (0, 1):
        where = [jax.random.randint(jax.random.fold_in(key, axis), (), 0, length) for axis, length in enumerate(entries.shape)]
        where[longest] = (where[longest] + shift) % entries.shape[longest]
        spots.append(tuple(where))
    return entries.at[spots[0]].set(smallest).at[spots[1]].set(top_value)


def level_of(key, shape, split, least, top_value):
    gain, own = 1.0, jax.random.fold_in(key, 6)
    for axis_at, blocks in split:
        draws = jnp.exp(jax.random.uniform(jax.random.fold_in(own, axis_at), (blocks,), jnp.float32, least / len(split), top_value / len(split)))
        gain = gain * jnp.repeat(draws, shape[axis_at] // blocks).reshape([-1 if axis == axis_at else 1 for axis in range(len(shape))])
    return gain


def centred(key, dims, width, limit, cuts=(), kind=jnp.bfloat16):
    values = jax.random.normal(key, dims, jnp.float32) * width
    if len(cuts) > 0:
        values = level_of(key, dims, cuts, -0.22, 0.18) * values
    return jnp.clip(values, min=-limit, max=limit).astype(kind)


def setup_inputs(seed: int = 0) -> dict:
    seeds = jax.random.split(jax.random.key(seed), 6)
    return {
        "query_block": draw_query_block(jax.random.fold_in(seeds[5], 71), 0),
        "k_cache": draw_k_cache(jax.random.fold_in(seeds[5], 71), 0),
        "v_cache": centred(seeds[2], (REQUESTS, CONTEXT, HK * DH), 1.0, 6.0, ((0, 32), (1, 16))),
        "ctx_len": draw_ctx_len(jax.random.fold_in(seeds[5], 71), 0),
        "host": set_ends(jax.random.randint(seeds[4], (REQUESTS,), 0, N_SEQ), jax.random.fold_in(seeds[4], 1), 0, N_SEQ - 1).astype(jnp.int32),
    }


NEG_FILL = -1e+30

def one_request(args):
    block_all, keys, values, length, root = args
    group = HQ // HK
    block = lax.dynamic_index_in_dim(block_all, root.astype(jnp.int32), 0, keepdims=False)
    queries = block[:, :HQ * DH].reshape(Q, HK, group, DH).astype(jnp.float32)
    new_keys = block[:, HQ * DH:(HQ + HK) * DH].reshape(Q, HK, DH).astype(jnp.float32)
    new_values = block[:, (HQ + HK) * DH:].reshape(Q, HK, DH).astype(jnp.float32)
    ctx_keys = keys.reshape(CONTEXT, HK, DH).astype(jnp.float32)
    ctx_values = values.reshape(N_SEQ, CTX_DEV, HK, DH).astype(jnp.float32)
    scale = 1.0 / math.sqrt(DH)
    ctx_scores = jnp.einsum('qhgd,khd->hgqk', queries, ctx_keys) * scale
    ctx_scores = ctx_scores.reshape(HK, group, Q, N_SEQ, CTX_DEV)
    new_scores = jnp.einsum('qhgd,khd->hgqk', queries, new_keys) * scale
    valid = (jnp.arange(CONTEXT, dtype=jnp.int32) < length).reshape(N_SEQ, CTX_DEV)
    causal = jnp.arange(Q)[:, None] >= jnp.arange(Q)[None, :]
    ctx_masked = jnp.where(valid, ctx_scores, NEG_FILL)
    new_masked = jnp.where(causal, new_scores, NEG_FILL)
    ctx_top = lax.optimization_barrier(jnp.max(ctx_masked, axis=-1))
    new_top = lax.optimization_barrier(jnp.max(new_masked, axis=-1))
    top = jnp.maximum(lax.optimization_barrier(jnp.max(ctx_top, axis=-1)), new_top)
    ctx_weights = jnp.where(valid, jnp.exp(ctx_masked - ctx_top[..., None]), 0.0)
    new_weights = jnp.where(causal, jnp.exp(new_masked - new_top[..., None]), 0.0)
    ctx_factor = jnp.exp(ctx_top - top[..., None])
    new_factor = jnp.exp(new_top - top)
    total = lax.optimization_barrier(jnp.sum(lax.optimization_barrier(jnp.sum(ctx_weights, axis=-1)) * ctx_factor, axis=-1)) + lax.optimization_barrier(jnp.sum(new_weights, axis=-1)) * new_factor
    ctx_round = ctx_weights.astype(jnp.bfloat16).astype(jnp.float32)
    new_round = new_weights.astype(jnp.bfloat16).astype(jnp.float32)
    ctx_part = jnp.einsum('hgqbk,bkhd->hgqbd', ctx_round, ctx_values)
    summed = lax.optimization_barrier(jnp.sum(ctx_part * ctx_factor[..., None], axis=3))
    summed = summed + jnp.einsum('hgqk,khd->hgqd', new_round, new_values) * new_factor[..., None]
    result = summed / total[..., None]
    result = jnp.transpose(result, (2, 0, 1, 3)).reshape(Q, HQ * DH).astype(jnp.bfloat16)
    slots = jnp.arange(N_SEQ, dtype=jnp.int32)[:, None, None] == root
    return jnp.where(slots, result[None], jnp.zeros((), jnp.bfloat16))

def reference(query_block, k_cache, v_cache, ctx_len, host):
    return lax.map(one_request, (query_block, k_cache, v_cache, ctx_len, host))
```

```python
import functools
import math

import jax
import jax.numpy as jnp
from jax import lax
from jax.experimental import pallas as pl
from jax.experimental.pallas import tpu as pltpu
from jax.sharding import PartitionSpec as P

HQ = 64
HK = 8
DH = 128
ROWS = 64
NY = 4
CHUNKS = 4
HP = 2
PIECE = HP * DH
LANES = HP * ROWS
HALF = NY * LANES
HALF_COLS = NY * PIECE
CHUNK_COLS = 2 * HALF_COLS
UNIT = 256
SCALE2 = math.log2(math.e) / math.sqrt(DH)
NEG = -1e30
FLOOR = -1e20
ABSENT = -2e20

CORE_Q, Y_Q, Z_Q, Y_QALL, CORE_QALL, CORE_O, Y_O, Z_O, Y_OALL, CORE_OALL = 0, 1, 4, 5, 8, 9, 10, 13, 14, 17
STAGES = 18


def three_parts(x):
    high = x.astype(jnp.bfloat16).astype(jnp.float32)
    rest = x - high
    mid = rest.astype(jnp.bfloat16).astype(jnp.float32)
    low = (rest - mid).astype(jnp.bfloat16).astype(jnp.float32)
    return high, mid, low


def pack_stats(top, total):
    width = top.shape[1]
    row = lax.broadcasted_iota(jnp.int32, (16, width), 0)
    out = jnp.zeros((16, width), jnp.float32)
    for at, part in enumerate(three_parts(top) + three_parts(total)):
        out = jnp.where(row == at, part, out)
    return out.astype(jnp.bfloat16)


def unpack_stats(packed):
    s = packed.astype(jnp.float32)
    return s[0:1] + s[1:2] + s[2:3], s[3:4] + s[4:5] + s[5:6]


def merge(parts):
    top = functools.reduce(jnp.maximum, [p[0] for p in parts])
    factors = [jnp.exp2((p[0] - top) * SCALE2) for p in parts]
    total = functools.reduce(jnp.add, [p[1] * f for p, f in zip(parts, factors)])
    summed = functools.reduce(jnp.add, [p[2] * f for p, f in zip(parts, factors)])
    return top, total, summed


def block_attention(keys, values, queries, keep):
    scores = lax.dot_general(keys, queries, (((1,), (1,)), ((), ())), preferred_element_type=jnp.float32)
    scores = jnp.where(keep, scores, NEG)
    top = jnp.maximum(jnp.max(scores, axis=0, keepdims=True), FLOOR)
    weights = jnp.exp2((scores - top) * SCALE2)
    total = jnp.sum(weights, axis=0, keepdims=True)
    summed = lax.dot_general(
        values, weights.astype(jnp.bfloat16), (((0,), (0,)), ((), ())), preferred_element_type=jnp.float32
    )
    return top, total, summed


def kernel(
    ctx_ref, host_ref, q_hbm, k_hbm, v_hbm, o_hbm,
    q_all, k_all, v_all, core_q, y_src, y_q, z_q, q_full,
    new_sum, new_stats, o_src, o_core, kept, y_osrc, y_o, half_o, z_osrc, z_o, o_full,
    local_sem, send_sem, recv_sem,
):
    context = k_hbm.shape[0]
    seq = lax.axis_index("seq")
    core = lax.rem(seq, 2)
    zhi = lax.rem(lax.div(seq, 2), 2)
    y = lax.div(seq, 4)
    other = 1 - core
    sibling = seq + 1 - 2 * core
    across = seq + 2 - 4 * zhi

    host = host_ref[0]
    host_core = lax.rem(host, 2)
    host_z = lax.rem(lax.div(host, 2), 2)
    host_y = lax.div(host, 4)

    def pick(index, values):
        out = values[0]
        for at in range(1, len(values)):
            out = lax.select(index == at, values[at], out)
        return out

    def cols(start, size):
        return pl.ds(pl.multiple_of(start, 128), size)

    def y_of(k):
        return lax.rem(y + k, NY)

    def beside(k):
        return lax.rem(seq + 4 * k, 16)

    def remote(src, dst, stage, s, to):
        return pltpu.make_async_remote_copy(
            src_ref=src,
            dst_ref=dst,
            send_sem=send_sem.at[stage, s],
            recv_sem=recv_sem.at[stage, s],
            device_id={"seq": to},
            device_id_type=pl.DeviceIdType.MESH,
        )

    def send_core_q(s):
        return remote(
            q_hbm.at[:, cols(s * CHUNK_COLS + other * HALF_COLS, HALF_COLS)], core_q.at[s, core], CORE_Q, s, sibling
        )

    def send_y_q(s, k):
        return remote(y_src.at[s, y_of(k)], y_q.at[s, y], Y_Q + k - 1, s, beside(k))

    def send_z_q(s):
        return remote(z_q.at[s, zhi], z_q.at[s, zhi], Z_Q, s, across)

    def send_y_qall(s, k):
        piece = core * NY + y
        return remote(q_full.at[s, piece], q_full.at[s, piece], Y_QALL + k - 1, s, beside(k))

    def send_core_qall(s):
        pieces = q_full.at[s, pl.ds(core * NY, NY)]
        return remote(pieces, pieces, CORE_QALL, s, sibling)

    def send_core_o(s):
        return remote(o_src.at[s], o_core.at[s], CORE_O, s, sibling)

    def send_y_o(s, k):
        return remote(y_osrc.at[s, y_of(k)], y_o.at[s, y], Y_O + k - 1, s, beside(k))

    def send_z_o(s):
        return remote(z_osrc.at[s], z_o.at[s], Z_O, s, across)

    def send_y_oall(s, k):
        piece = o_full.at[s, :, cols((other * NY + y) * PIECE, PIECE)]
        return remote(piece, piece, Y_OALL + k - 1, s, beside(k))

    def send_core_oall(s):
        pieces = o_full.at[s, :, cols(other * HALF_COLS, HALF_COLS)]
        return remote(pieces, pieces, CORE_OALL, s, sibling)

    def write_out(s):
        return pltpu.make_async_copy(o_full.at[s], o_hbm.at[:, cols(s * CHUNK_COLS, CHUNK_COLS)], local_sem.at[4 + s])

    def own_q(s):
        return pltpu.make_async_copy(
            q_hbm.at[:, cols(s * CHUNK_COLS + core * HALF_COLS, HALF_COLS)], core_q.at[s, core], local_sem.at[4 + s]
        )

    loads = [
        pltpu.make_async_copy(src, dst, local_sem.at[at])
        for at, (src, dst) in enumerate(((q_hbm, q_all), (k_hbm, k_all), (v_hbm, v_all)))
    ]
    for s in range(CHUNKS):
        own_q(s).start()
    for copy in loads:
        copy.start()

    barrier = pltpu.get_barrier_semaphore()
    for to in (across, beside(2), beside(1), beside(3), sibling):
        pl.semaphore_signal(barrier, inc=1, device_id={"seq": to}, device_id_type=pl.DeviceIdType.MESH)
    pl.semaphore_wait(barrier, 5)

    @pl.loop(0, CHUNKS)
    def _(s):
        send_core_q(s).start()

    @pl.loop(0, CHUNKS)
    def _(s):
        own_q(s).wait()
        send_core_q(s).wait_recv()
        for at in range(NY):
            piece = slice(at * PIECE, (at + 1) * PIECE)
            y_src[s, at] = pick(host_core, [core_q[s, c, :, piece] for c in range(2)])
        for k in (2, 1, 3):
            send_y_q(s, k).start()
        y_q[s, y] = y_src[s, y]

    @pl.loop(0, CHUNKS)
    def _(s):
        for k in (1, 3, 2):
            send_y_q(s, k).wait_recv()
        z_q[s, zhi] = pick(host_y, [y_q[s, at] for at in range(NY)])
        send_z_q(s).start()

    for copy in loads:
        copy.wait()
    is_host = jnp.broadcast_to(host, (1, HALF)) == jnp.broadcast_to(seq, (1, HALF))
    causal = lax.broadcasted_iota(jnp.int32, (ROWS, HALF), 0) <= lax.rem(
        lax.broadcasted_iota(jnp.int32, (ROWS, HALF), 1), ROWS
    )

    @pl.loop(0, HK)
    def _(g):
        queries = jnp.concatenate(
            [q_all[:, cols(g * HALF_COLS + h * DH, DH)] for h in range(HQ // HK)], axis=0
        )
        new_keys = q_all[:, cols(HQ * DH + g * DH, DH)]
        new_values = q_all[:, cols((HQ + HK) * DH + g * DH, DH)]
        top, total, summed = block_attention(new_keys, new_values, queries, causal)
        new_sum[g] = summed
        new_stats[g, 0:1] = jnp.where(is_host, top, ABSENT)
        new_stats[g, 1:2] = total

    valid = ctx_ref[0] - seq * context

    def attend(s, half, unit):
        g = 2 * s + half
        at = unit * UNIT
        keys = k_all[:, cols(g * DH, DH)]
        values = v_all[:, cols(g * DH, DH)]
        heads = range(at // ROWS, (at + UNIT) // ROWS)
        queries = jnp.concatenate(
            [q_full[s, half * NY + h // HP, :, (h % HP) * DH : (h % HP + 1) * DH] for h in heads], axis=0
        )
        keep = lax.broadcasted_iota(jnp.int32, (context, UNIT), 0) < valid
        here = block_attention(keys, values, queries, keep)
        new = (new_stats[g, 0:1, at : at + UNIT], new_stats[g, 1:2, at : at + UNIT], new_sum[g, :, at : at + UNIT])
        return merge([here, new])

    def gather_q(s):
        send_z_q(s).wait_recv()
        q_full[s, core * NY + y] = pick(host_z, [z_q[s, at] for at in range(2)])
        for k in (2, 1, 3):
            send_y_qall(s, k).start()

    def compute(s):
        for k in (1, 3, 2):
            send_y_qall(s, k).wait_recv()
        send_core_qall(s).start()
        for unit in range(HALF // UNIT):
            top, total, summed = attend(s, core, unit)
            at = unit * UNIT
            o_src[s, 0:DH, at : at + UNIT] = summed
            o_src[s, DH : DH + 1, at : at + UNIT] = top
            o_src[s, DH + 1 : DH + 2, at : at + UNIT] = total
        send_core_o(s).start()
        send_core_qall(s).wait_recv()
        mine = [attend(s, other, unit) for unit in range(HALF // UNIT)]
        send_core_o(s).wait_recv()
        for unit, part in enumerate(mine):
            at = unit * UNIT
            beside_it = (
                o_core[s, DH : DH + 1, at : at + UNIT],
                o_core[s, DH + 1 : DH + 2, at : at + UNIT],
                o_core[s, 0:DH, at : at + UNIT],
            )
            top, total, summed = merge([part, beside_it])
            packed = pack_stats(top, total)
            for sub in range(UNIT // LANES):
                lanes = slice(sub * LANES, (sub + 1) * LANES)
                piece = unit * (UNIT // LANES) + sub
                y_osrc[s, piece, 0:DH] = summed[:, lanes].astype(jnp.bfloat16)
                y_osrc[s, piece, DH : DH + 16] = packed[:, lanes]
                kept[s, piece, 0:DH] = summed[:, lanes]
                kept[s, piece, DH : DH + 1] = top[:, lanes]
                kept[s, piece, DH + 1 : DH + 2] = total[:, lanes]
        for k in (2, 1, 3):
            send_y_o(s, k).start()

    def arrived(ref, *at):
        top, total = unpack_stats(ref[(*at, slice(DH, DH + 16))])
        return top, total, ref[(*at, slice(0, DH))].astype(jnp.float32)

    def sum_y(s):
        for k in (1, 3, 2):
            send_y_o(s, k).wait_recv()
        own = (kept[s, y, DH : DH + 1], kept[s, y, DH + 1 : DH + 2], kept[s, y, 0:DH])
        top, total, summed = merge([own] + [arrived(y_o, s, y_of(k)) for k in (1, 2, 3)])
        z_osrc[s, 0:DH] = summed.astype(jnp.bfloat16)
        z_osrc[s, DH : DH + 16] = pack_stats(top, total)
        send_z_o(s).start()
        half_o[s, 0:DH] = summed
        half_o[s, DH : DH + 1] = top
        half_o[s, DH + 1 : DH + 2] = total

    @pl.loop(0, CHUNKS + 3)
    def _(t):
        @pl.when(t < CHUNKS)
        def _():
            gather_q(t)

        @pl.when((t >= 1) & (t <= CHUNKS))
        def _():
            compute(t - 1)

        @pl.when(t >= 3)
        def _():
            sum_y(t - 3)

    def finish(s):
        send_z_o(s).wait_recv()
        own = (half_o[s, DH : DH + 1], half_o[s, DH + 1 : DH + 2], half_o[s, 0:DH])
        _, total, summed = merge([own, arrived(z_o, s)])
        result = jnp.transpose(summed / total).astype(jnp.bfloat16)
        for h in range(HP):
            o_full[s, :, cols((other * NY + y) * PIECE + h * DH, DH)] = result[h * ROWS : (h + 1) * ROWS]
        for k in (2, 1, 3):
            send_y_oall(s, k).start()

    def gather_o(s):
        for k in (1, 3, 2):
            send_y_oall(s, k).wait_recv()
        send_core_oall(s).start()
        send_core_oall(s).wait_recv()
        write_out(s).start()

    @pl.loop(0, CHUNKS + 1)
    def _(t):
        @pl.when(t < CHUNKS)
        def _():
            finish(t)

        @pl.when(t >= 1)
        def _():
            gather_o(t - 1)

    @pl.loop(0, CHUNKS)
    def _(s):
        for copy in (send_core_q, send_z_q, send_core_qall, send_core_o, send_z_o, send_core_oall):
            copy(s).wait_send()
        for copy in (send_y_q, send_y_qall, send_y_o, send_y_oall):
            for k in (1, 2, 3):
                copy(s, k).wait_send()
        write_out(s).wait()


def attention(query_block, keys, values, ctx_len, host):
    context, width = keys.shape
    bf16, f32 = jnp.bfloat16, jnp.float32
    vmem = pltpu.VMEM
    return pl.pallas_call(
        kernel,
        out_shape=jax.ShapeDtypeStruct((ROWS, HQ * DH), bf16),
        in_specs=[pl.BlockSpec(memory_space=pltpu.SMEM)] * 2 + [pl.BlockSpec(memory_space=pl.ANY)] * 3,
        out_specs=pl.BlockSpec(memory_space=pl.ANY),
        scratch_shapes=[
            vmem(query_block.shape, bf16),
            vmem((context, width), bf16),
            vmem((context, width), bf16),
            vmem((CHUNKS, 2, ROWS, HALF_COLS), bf16),
            vmem((CHUNKS, NY, ROWS, PIECE), bf16),
            vmem((CHUNKS, NY, ROWS, PIECE), bf16),
            vmem((CHUNKS, 2, ROWS, PIECE), bf16),
            vmem((CHUNKS, 2 * NY, ROWS, PIECE), bf16),
            vmem((HK, DH, HALF), f32),
            vmem((HK, 8, HALF), f32),
            vmem((CHUNKS, DH + 8, HALF), f32),
            vmem((CHUNKS, DH + 8, HALF), f32),
            vmem((CHUNKS, NY, DH + 8, LANES), f32),
            vmem((CHUNKS, NY, DH + 16, LANES), bf16),
            vmem((CHUNKS, NY, DH + 16, LANES), bf16),
            vmem((CHUNKS, DH + 8, LANES), f32),
            vmem((CHUNKS, DH + 16, LANES), bf16),
            vmem((CHUNKS, DH + 16, LANES), bf16),
            vmem((CHUNKS, ROWS, CHUNK_COLS), bf16),
            pltpu.SemaphoreType.DMA((4 + CHUNKS,)),
            pltpu.SemaphoreType.DMA((STAGES, CHUNKS)),
            pltpu.SemaphoreType.DMA((STAGES, CHUNKS)),
        ],
        compiler_params=pltpu.CompilerParams(
            collective_id=0, has_side_effects=True, vmem_limit_bytes=52 * 1024 * 1024
        ),
        name="context_attention",
    )(ctx_len, host, query_block, keys, values)


def local(query_block, k_cache, v_cache, ctx_len, host):
    result = attention(query_block[0, 0], k_cache[0], v_cache[0], ctx_len, host)
    result = jnp.where(lax.axis_index("seq") == host[0], result, jnp.zeros((), jnp.bfloat16))
    return result[None, None]


def solution(mesh):
    return jax.shard_map(
        local,
        mesh=mesh,
        in_specs=(
            P("req", "seq", None, None),
            P("req", "seq", None),
            P("req", "seq", None),
            P("req"),
            P("req"),
        ),
        out_specs=P("req", "seq", None, None),
        check_vma=False,
    )
```

```python
import functools
import math

import jax
import jax.numpy as jnp
from jax import lax
from jax.experimental import pallas as pl
from jax.experimental.pallas import tpu as pltpu
from jax.sharding import PartitionSpec as P

HQ = 64
HK = 8
DH = 128
ROWS = 64
NY = 4
CHUNKS = 8
HALF_COLS = HQ // HK * DH // 2
CHUNK_COLS = 2 * HALF_COLS
LANES = 256
BLOCK = 128
DEPTH = DH // 2
SCALE2 = math.log2(math.e) / math.sqrt(DH)
NEG = -1e30
FLOOR = -1e20
ABSENT = -2e20

CORE_Q, Y_Q, Z_Q, Y_QALL, CORE_QALL, CORE_O, Y_O, Z_O, Y_OALL, CORE_OALL = 0, 1, 4, 5, 8, 9, 10, 13, 14, 17
STAGES = 18

AT_NEAR, AT_FAR, AT_SUM, AT_FINISH, AT_GATHER, AT_WRITE = 4, 5, 8, 16, 20, 22


def three_parts(x):
    high = x.astype(jnp.bfloat16).astype(jnp.float32)
    rest = x - high
    mid = rest.astype(jnp.bfloat16).astype(jnp.float32)
    low = (rest - mid).astype(jnp.bfloat16).astype(jnp.float32)
    return high, mid, low


def pack_stats(top, total):
    width = top.shape[1]
    row = lax.broadcasted_iota(jnp.int32, (16, width), 0)
    out = jnp.zeros((16, width), jnp.float32)
    for at, part in enumerate(three_parts(top) + three_parts(total)):
        out = jnp.where(row == at, part, out)
    return out.astype(jnp.bfloat16)


def unpack_stats(packed):
    s = packed.astype(jnp.float32)
    return s[0:1] + s[1:2] + s[2:3], s[3:4] + s[4:5] + s[5:6]


def merge(parts):
    top = functools.reduce(jnp.maximum, [p[0] for p in parts])
    factors = [jnp.exp2((p[0] - top) * SCALE2) for p in parts]
    total = functools.reduce(jnp.add, [p[1] * f for p, f in zip(parts, factors)])
    summed = functools.reduce(jnp.add, [p[2] * f for p, f in zip(parts, factors)])
    return top, total, summed


def weigh(keys, queries, keep):
    scores = lax.dot_general(keys, queries, (((1,), (1,)), ((), ())), preferred_element_type=jnp.float32)
    scores = jnp.where(keep, scores, NEG)
    top = jnp.maximum(jnp.max(scores, axis=0, keepdims=True), FLOOR)
    weights = jnp.exp2((scores - top) * SCALE2)
    return top, jnp.sum(weights, axis=0, keepdims=True), weights.astype(jnp.bfloat16)


def kernel(
    ctx_ref, host_ref, q_hbm, k_hbm, v_hbm, o_hbm,
    q_all, k_all, v_all, v_turned, core_q, y_src, y_q, z_q, q_full,
    new_sum, new_stats, o_src, o_core, kept, y_osrc, y_o, half_o, z_osrc, z_o, o_pieces, o_full,
    local_sem, send_sem, recv_sem,
):
    context = k_hbm.shape[0]
    seq = lax.axis_index("seq")
    core = lax.rem(seq, 2)
    zhi = lax.rem(lax.div(seq, 2), 2)
    y = lax.div(seq, 4)
    other = 1 - core
    sibling = seq + 1 - 2 * core
    across = seq + 2 - 4 * zhi

    host = host_ref[0]
    host_core = lax.rem(host, 2)
    host_z = lax.rem(lax.div(host, 2), 2)
    host_y = lax.div(host, 4)

    def pick(index, values):
        out = values[0]
        for at in range(1, len(values)):
            out = lax.select(index == at, values[at], out)
        return out

    def cols(start, size):
        return pl.ds(pl.multiple_of(start, 128), size)

    def y_of(k):
        return lax.rem(y + k, NY)

    def beside(k):
        return lax.rem(seq + 4 * k, 16)

    def remote(src, dst, stage, s, to):
        return pltpu.make_async_remote_copy(
            src_ref=src,
            dst_ref=dst,
            send_sem=send_sem.at[stage, s],
            recv_sem=recv_sem.at[stage, s],
            device_id={"seq": to},
            device_id_type=pl.DeviceIdType.MESH,
        )

    def send_core_q(s):
        return remote(
            q_hbm.at[:, cols(s * CHUNK_COLS + other * HALF_COLS, HALF_COLS)], core_q.at[s, core], CORE_Q, s, sibling
        )

    def send_y_q(s, k):
        return remote(y_src.at[s, y_of(k)], y_q.at[s, y], Y_Q + k - 1, s, beside(k))

    def send_z_q(s):
        return remote(z_q.at[s, zhi], z_q.at[s, zhi], Z_Q, s, across)

    def send_y_qall(s, k):
        piece = q_full.at[s, core, y]
        return remote(piece, piece, Y_QALL + k - 1, s, beside(k))

    def send_core_qall(s):
        return remote(q_full.at[s, core], q_full.at[s, core], CORE_QALL, s, sibling)

    def send_core_o(s):
        return remote(o_src.at[s], o_core.at[s], CORE_O, s, sibling)

    def send_y_o(s, k):
        return remote(y_osrc.at[s, y_of(k)], y_o.at[s, y], Y_O + k - 1, s, beside(k))

    def send_z_o(s):
        return remote(z_osrc.at[s], z_o.at[s], Z_O, s, across)

    def send_y_oall(s, k):
        piece = o_pieces.at[s, other, y]
        return remote(piece, piece, Y_OALL + k - 1, s, beside(k))

    def send_core_oall(s):
        return remote(o_pieces.at[s, other], o_pieces.at[s, other], CORE_OALL, s, sibling)

    def write_out(s):
        return pltpu.make_async_copy(o_full.at[s], o_hbm.at[:, cols(s * CHUNK_COLS, CHUNK_COLS)], local_sem.at[4 + s])

    def own_q(s):
        return pltpu.make_async_copy(
            q_hbm.at[:, cols(s * CHUNK_COLS + core * HALF_COLS, HALF_COLS)], core_q.at[s, core], local_sem.at[4 + s]
        )

    loads = [
        pltpu.make_async_copy(src, dst, local_sem.at[at])
        for at, (src, dst) in enumerate(((q_hbm, q_all), (k_hbm, k_all), (v_hbm, v_all)))
    ]
    barrier = pltpu.get_barrier_semaphore()

    def greet(to):
        pl.semaphore_signal(barrier, inc=1, device_id={"seq": to}, device_id_type=pl.DeviceIdType.MESH)

    for to in (beside(2), beside(1), beside(3), sibling):
        greet(to)
    for s in range(CHUNKS):
        own_q(s).start()
    for copy in loads:
        copy.start()

    @pl.when(zhi == 0)
    def _():
        pl.semaphore_wait(barrier, 4)
        greet(across)

    @pl.when(zhi == 1)
    def _():
        pl.semaphore_wait(barrier, 5)
        greet(across)

    @pl.loop(0, CHUNKS)
    def _(s):
        send_core_q(s).start()

    @pl.loop(0, CHUNKS)
    def _(s):
        own_q(s).wait()
        send_core_q(s).wait_recv()
        for at in range(NY):
            piece = slice(at * DH, (at + 1) * DH)
            y_src[s, at] = pick(host_core, [core_q[s, c, :, piece] for c in range(2)])
        for k in (2, 1, 3):
            send_y_q(s, k).start()
        y_q[s, y] = y_src[s, y]

    for copy in loads:
        copy.wait()
    is_host = jnp.broadcast_to(host, (1, 2 * LANES)) == jnp.broadcast_to(seq, (1, 2 * LANES))
    causal = lax.broadcasted_iota(jnp.int32, (ROWS, 2 * LANES), 0) <= lax.rem(
        lax.broadcasted_iota(jnp.int32, (ROWS, 2 * LANES), 1), ROWS
    )

    def new_tokens(g):
        queries = jnp.concatenate(
            [q_all[:, cols(g * CHUNK_COLS + h * DH, DH)] for h in range(HQ // HK)], axis=0
        )
        new_keys = q_all[:, cols(HQ * DH + g * DH, DH)]
        new_values = q_all[:, cols((HQ + HK) * DH + g * DH, DH)]
        top, total, weights = weigh(new_keys, queries, causal)
        summed = lax.dot_general(
            new_values, weights, (((0,), (0,)), ((), ())), preferred_element_type=jnp.float32
        )
        top = jnp.where(is_host, top, ABSENT)
        for half in range(2):
            lanes = slice(half * LANES, (half + 1) * LANES)
            new_sum[g, half] = summed[:, lanes]
            new_stats[g, half, 0:1] = top[:, lanes]
            new_stats[g, half, 1:2] = total[:, lanes]
        v_turned[g] = jnp.transpose(v_all[:, cols(g * DH, DH)])

    @pl.when(zhi == 0)
    def _():
        pl.semaphore_wait(barrier, 1)

    @pl.loop(0, CHUNKS)
    def _(s):
        for k in (1, 3, 2):
            send_y_q(s, k).wait_recv()
        z_q[s, zhi] = pick(host_y, [y_q[s, at] for at in range(NY)])
        send_z_q(s).start()
        new_tokens(s)

    valid = ctx_ref[0] - seq * context

    def attend(s, half):
        queries = jnp.concatenate([q_full[s, half, h] for h in range(NY)], axis=0)
        keep = lax.broadcasted_iota(jnp.int32, (context, LANES), 0) < valid
        top, total, weights = weigh(k_all[:, cols(s * DH, DH)], queries, keep)
        summed = jnp.dot(v_turned[s], weights, preferred_element_type=jnp.float32)
        new = (new_stats[s, half, 0:1], new_stats[s, half, 1:2], new_sum[s, half])
        return merge([(top, total, summed), new])

    def gather_q(s):
        send_z_q(s).wait_recv()
        q_full[s, core, y] = pick(host_z, [z_q[s, at] for at in range(2)])
        for k in (2, 1, 3):
            send_y_qall(s, k).start()

    def compute_near(s):
        for k in (1, 3, 2):
            send_y_qall(s, k).wait_recv()
        send_core_qall(s).start()
        top, total, summed = attend(s, core)
        o_src[s, 0:DH] = summed
        o_src[s, DH : DH + 1] = top
        o_src[s, DH + 1 : DH + 2] = total
        send_core_o(s).start()

    def compute_far(s):
        send_core_qall(s).wait_recv()
        part = attend(s, other)
        send_core_o(s).wait_recv()
        beside_it = (o_core[s, DH : DH + 1], o_core[s, DH + 1 : DH + 2], o_core[s, 0:DH])
        top, total, summed = merge([part, beside_it])
        packed = pack_stats(top, total)
        for piece in range(NY):
            block = piece // 2
            lanes = slice(block * BLOCK, (block + 1) * BLOCK)
            deep = summed[piece % 2 * DEPTH : (piece % 2 + 1) * DEPTH, lanes]
            y_osrc[s, piece, 0:DEPTH] = deep.astype(jnp.bfloat16)
            y_osrc[s, piece, DEPTH : DEPTH + 16] = packed[:, lanes]
            kept[s, piece, 0:DEPTH] = deep
            kept[s, piece, DEPTH : DEPTH + 1] = top[:, lanes]
            kept[s, piece, DEPTH + 1 : DEPTH + 2] = total[:, lanes]
        for k in (2, 1, 3):
            send_y_o(s, k).start()

    def arrived(ref, *at):
        top, total = unpack_stats(ref[(*at, slice(DEPTH, DEPTH + 16))])
        return top, total, ref[(*at, slice(0, DEPTH))].astype(jnp.float32)

    def sum_y(s):
        for k in (1, 3, 2):
            send_y_o(s, k).wait_recv()
        own = (kept[s, y, DEPTH : DEPTH + 1], kept[s, y, DEPTH + 1 : DEPTH + 2], kept[s, y, 0:DEPTH])
        top, total, summed = merge([own] + [arrived(y_o, s, y_of(k)) for k in (1, 2, 3)])
        z_osrc[s, 0:DEPTH] = summed.astype(jnp.bfloat16)
        z_osrc[s, DEPTH : DEPTH + 16] = pack_stats(top, total)
        send_z_o(s).start()
        half_o[s, 0:DEPTH] = summed
        half_o[s, DEPTH : DEPTH + 1] = top
        half_o[s, DEPTH + 1 : DEPTH + 2] = total

    def sent(single, along_y, s):
        for copy in single:
            copy(s).wait_send()
        for copy in along_y:
            for k in (1, 2, 3):
                copy(s, k).wait_send()

    def finish(s):
        sent((send_core_q, send_z_q, send_core_qall, send_core_o), (send_y_q, send_y_qall, send_y_o), s)
        send_z_o(s).wait_recv()
        own = (half_o[s, DEPTH : DEPTH + 1], half_o[s, DEPTH + 1 : DEPTH + 2], half_o[s, 0:DEPTH])
        _, total, summed = merge([own, arrived(z_o, s)])
        o_pieces[s, other, y] = (summed / total).astype(jnp.bfloat16)
        for k in (2, 1, 3):
            send_y_oall(s, k).start()

    def lay_out(s, half):
        for block in range(2):
            turned = jnp.transpose(
                jnp.concatenate([o_pieces[s, half, 2 * block + e].astype(jnp.float32) for e in range(2)], axis=0)
            ).astype(jnp.bfloat16)
            for h in range(2):
                o_full[s, :, cols(half * HALF_COLS + (2 * block + h) * DH, DH)] = turned[h * ROWS : (h + 1) * ROWS]

    def gather_o(s):
        for k in (1, 3, 2):
            send_y_oall(s, k).wait_recv()
        send_core_oall(s).start()
        lay_out(s, other)

    def write_o(s):
        send_core_oall(s).wait_recv()
        lay_out(s, core)
        write_out(s).start()
        sent((send_z_o, send_core_oall), (send_y_oall,), s)

    @pl.loop(0, CHUNKS + AT_WRITE)
    def _(t):
        for at, stage in (
            (0, gather_q),
            (AT_NEAR, compute_near),
            (AT_FAR, compute_far),
            (AT_SUM, sum_y),
            (AT_FINISH, finish),
            (AT_GATHER, gather_o),
            (AT_WRITE, write_o),
        ):
            pl.when((t >= at) & (t < at + CHUNKS))(functools.partial(stage, t - at))

    @pl.loop(0, CHUNKS)
    def _(s):
        write_out(s).wait()


def attention(query_block, keys, values, ctx_len, host):
    context, width = keys.shape
    bf16, f32 = jnp.bfloat16, jnp.float32
    vmem = pltpu.VMEM
    return pl.pallas_call(
        kernel,
        out_shape=jax.ShapeDtypeStruct((ROWS, HQ * DH), bf16),
        in_specs=[pl.BlockSpec(memory_space=pltpu.SMEM)] * 2 + [pl.BlockSpec(memory_space=pl.ANY)] * 3,
        out_specs=pl.BlockSpec(memory_space=pl.ANY),
        scratch_shapes=[
            vmem(query_block.shape, bf16),
            vmem((context, width), bf16),
            vmem((context, width), bf16),
            vmem((HK, DH, context), bf16),
            vmem((CHUNKS, 2, ROWS, HALF_COLS), bf16),
            vmem((CHUNKS, NY, ROWS, DH), bf16),
            vmem((CHUNKS, NY, ROWS, DH), bf16),
            vmem((CHUNKS, 2, ROWS, DH), bf16),
            vmem((CHUNKS, 2, NY, ROWS, DH), bf16),
            vmem((HK, 2, DH, LANES), f32),
            vmem((HK, 2, 8, LANES), f32),
            vmem((CHUNKS, DH + 8, LANES), f32),
            vmem((CHUNKS, DH + 8, LANES), f32),
            vmem((CHUNKS, NY, DEPTH + 8, BLOCK), f32),
            vmem((CHUNKS, NY, DEPTH + 16, BLOCK), bf16),
            vmem((CHUNKS, NY, DEPTH + 16, BLOCK), bf16),
            vmem((CHUNKS, DEPTH + 8, BLOCK), f32),
            vmem((CHUNKS, DEPTH + 16, BLOCK), bf16),
            vmem((CHUNKS, DEPTH + 16, BLOCK), bf16),
            vmem((CHUNKS, 2, NY, DEPTH, BLOCK), bf16),
            vmem((CHUNKS, ROWS, CHUNK_COLS), bf16),
            pltpu.SemaphoreType.DMA((4 + CHUNKS,)),
            pltpu.SemaphoreType.DMA((STAGES, CHUNKS)),
            pltpu.SemaphoreType.DMA((STAGES, CHUNKS)),
        ],
        compiler_params=pltpu.CompilerParams(
            collective_id=0, has_side_effects=True, vmem_limit_bytes=52 * 1024 * 1024
        ),
        name="context_attention",
    )(ctx_len, host, query_block, keys, values)


def local(query_block, k_cache, v_cache, ctx_len, host):
    result = attention(query_block[0, 0], k_cache[0], v_cache[0], ctx_len, host)
    result = jnp.where(lax.axis_index("seq") == host[0], result, jnp.zeros((), jnp.bfloat16))
    return result[None, None]


def solution(mesh):
    return jax.shard_map(
        local,
        mesh=mesh,
        in_specs=(
            P("req", "seq", None, None),
            P("req", "seq", None),
            P("req", "seq", None),
            P("req"),
            P("req"),
        ),
        out_specs=P("req", "seq", None, None),
        check_vma=False,
    )
```

```python
import functools
import math

import jax
import jax.numpy as jnp
from jax import lax
from jax.experimental import pallas as pl
from jax.experimental.pallas import tpu as pltpu
from jax.sharding import PartitionSpec as P

HQ = 64
HK = 8
DH = 128
ROWS = 64
NY = 4
CHUNKS = 8
HALF_COLS = HQ // HK * DH // 2
CHUNK_COLS = 2 * HALF_COLS
LANES = 256
BLOCK = 128
DEPTH = DH // 2
SCALE2 = math.log2(math.e) / math.sqrt(DH)
NEG = -1e30
FLOOR = -1e20
ABSENT = -2e20

CORE_Q, Y_Q, Z_Q, Y_QALL, CORE_QALL, CORE_O, Y_O, Z_O, Y_OALL, CORE_OALL = 0, 1, 4, 5, 8, 9, 10, 13, 14, 17
STAGES = 18
AHEAD = 4

AT_NEAR, AT_FAR, AT_SUM, AT_FINISH, AT_GATHER, AT_WRITE = 4, 5, 8, 18, 24, 26


def three_parts(x):
    high = x.astype(jnp.bfloat16).astype(jnp.float32)
    rest = x - high
    mid = rest.astype(jnp.bfloat16).astype(jnp.float32)
    low = (rest - mid).astype(jnp.bfloat16).astype(jnp.float32)
    return high, mid, low


def pack_stats(top, total):
    width = top.shape[1]
    row = lax.broadcasted_iota(jnp.int32, (16, width), 0)
    out = jnp.zeros((16, width), jnp.float32)
    for at, part in enumerate(three_parts(top) + three_parts(total)):
        out = jnp.where(row == at, part, out)
    return out.astype(jnp.bfloat16)


def unpack_stats(packed):
    s = packed.astype(jnp.float32)
    return s[0:1] + s[1:2] + s[2:3], s[3:4] + s[4:5] + s[5:6]


def merge(parts):
    top = functools.reduce(jnp.maximum, [p[0] for p in parts])
    factors = [jnp.exp2((p[0] - top) * SCALE2) for p in parts]
    total = functools.reduce(jnp.add, [p[1] * f for p, f in zip(parts, factors)])
    summed = functools.reduce(jnp.add, [p[2] * f for p, f in zip(parts, factors)])
    return top, total, summed


def weigh(keys, queries, keep):
    scores = lax.dot_general(keys, queries, (((1,), (1,)), ((), ())), preferred_element_type=jnp.float32)
    scores = jnp.where(keep, scores, NEG)
    top = jnp.maximum(jnp.max(scores, axis=0, keepdims=True), FLOOR)
    weights = jnp.exp2((scores - top) * SCALE2)
    return top, jnp.sum(weights, axis=0, keepdims=True), weights.astype(jnp.bfloat16)


def kernel(
    ctx_ref, host_ref, q_hbm, k_hbm, v_hbm, o_ref,
    q_all, k_all, v_all, v_turned, core_q, y_src, y_q, z_q, q_full,
    new_sum, new_stats, o_src, o_core, kept, y_osrc, y_o, half_o, z_osrc, z_o, o_pieces,
    local_sem, send_sem, recv_sem,
):
    context = k_hbm.shape[0]
    seq = lax.axis_index("seq")
    core = lax.rem(seq, 2)
    zhi = lax.rem(lax.div(seq, 2), 2)
    y = lax.div(seq, 4)
    other = 1 - core
    sibling = seq + 1 - 2 * core
    across = seq + 2 - 4 * zhi

    host = host_ref[0]
    host_core = lax.rem(host, 2)
    host_z = lax.rem(lax.div(host, 2), 2)
    host_y = lax.div(host, 4)

    def pick(index, values):
        out = values[0]
        for at in range(1, len(values)):
            out = lax.select(index == at, values[at], out)
        return out

    def cols(start, size):
        return pl.ds(pl.multiple_of(start, 128), size)

    def y_of(k):
        return lax.rem(y + k, NY)

    def beside(k):
        return lax.rem(seq + 4 * k, 16)

    def remote(src, dst, stage, s, to):
        return pltpu.make_async_remote_copy(
            src_ref=src,
            dst_ref=dst,
            send_sem=send_sem.at[stage, s],
            recv_sem=recv_sem.at[stage, s],
            device_id={"seq": to},
            device_id_type=pl.DeviceIdType.MESH,
        )

    def send_core_q(s):
        return remote(
            q_hbm.at[:, cols(s * CHUNK_COLS + other * HALF_COLS, HALF_COLS)], core_q.at[s, core], CORE_Q, s, sibling
        )

    def send_y_q(s, k):
        return remote(y_src.at[s, y_of(k)], y_q.at[s, y], Y_Q + k - 1, s, beside(k))

    def send_z_q(s):
        return remote(z_q.at[s, zhi], z_q.at[s, zhi], Z_Q, s, across)

    def send_y_qall(s, k):
        piece = q_full.at[s, core, y]
        return remote(piece, piece, Y_QALL + k - 1, s, beside(k))

    def send_core_qall(s):
        return remote(q_full.at[s, core], q_full.at[s, core], CORE_QALL, s, sibling)

    def send_core_o(s):
        return remote(o_src.at[s], o_core.at[s], CORE_O, s, sibling)

    def send_y_o(s, k):
        return remote(y_osrc.at[s, y_of(k)], y_o.at[s, y], Y_O + k - 1, s, beside(k))

    def send_z_o(s):
        return remote(z_osrc.at[s], z_o.at[s], Z_O, s, across)

    def send_y_oall(s, k):
        piece = o_pieces.at[s, other, y]
        return remote(piece, piece, Y_OALL + k - 1, s, beside(k))

    def send_core_oall(s):
        return remote(o_pieces.at[s, other], o_pieces.at[s, other], CORE_OALL, s, sibling)

    def own_q(s):
        return pltpu.make_async_copy(
            q_hbm.at[:, cols(s * CHUNK_COLS + core * HALF_COLS, HALF_COLS)], core_q.at[s, core], local_sem.at[4 + s]
        )

    loads = [
        pltpu.make_async_copy(src, dst, local_sem.at[at])
        for at, (src, dst) in enumerate(((q_hbm, q_all), (k_hbm, k_all), (v_hbm, v_all)))
    ]
    barrier = pltpu.get_barrier_semaphore()

    def greet(to):
        pl.semaphore_signal(barrier, inc=1, device_id={"seq": to}, device_id_type=pl.DeviceIdType.MESH)

    for to in (beside(2), beside(1), beside(3), sibling):
        greet(to)
    for s in range(CHUNKS):
        own_q(s).start()
    for copy in loads:
        copy.start()

    @pl.when(zhi == 0)
    def _():
        pl.semaphore_wait(barrier, 4)
        greet(across)

    @pl.when(zhi == 1)
    def _():
        pl.semaphore_wait(barrier, 5)
        greet(across)

    @pl.loop(0, CHUNKS)
    def _(s):
        send_core_q(s).start()

    def turn_q(s):
        own_q(s).wait()
        send_core_q(s).wait_recv()
        for at in range(NY):
            piece = slice(at * DH, (at + 1) * DH)
            y_src[s, at] = pick(host_core, [core_q[s, c, :, piece] for c in range(2)])
        for k in (2, 1, 3):
            send_y_q(s, k).start()
        y_q[s, y] = y_src[s, y]

    pl.loop(0, AHEAD)(turn_q)

    for copy in loads:
        copy.wait()
    is_host = jnp.broadcast_to(host, (1, 2 * LANES)) == jnp.broadcast_to(seq, (1, 2 * LANES))
    causal = lax.broadcasted_iota(jnp.int32, (ROWS, 2 * LANES), 0) <= lax.rem(
        lax.broadcasted_iota(jnp.int32, (ROWS, 2 * LANES), 1), ROWS
    )

    def new_tokens(g):
        queries = jnp.concatenate(
            [q_all[:, cols(g * CHUNK_COLS + h * DH, DH)] for h in range(HQ // HK)], axis=0
        )
        new_keys = q_all[:, cols(HQ * DH + g * DH, DH)]
        new_values = q_all[:, cols((HQ + HK) * DH + g * DH, DH)]
        top, total, weights = weigh(new_keys, queries, causal)
        summed = lax.dot_general(
            new_values, weights, (((0,), (0,)), ((), ())), preferred_element_type=jnp.float32
        )
        top = jnp.where(is_host, top, ABSENT)
        for half in range(2):
            lanes = slice(half * LANES, (half + 1) * LANES)
            new_sum[g, half] = summed[:, lanes]
            new_stats[g, half, 0:1] = top[:, lanes]
            new_stats[g, half, 1:2] = total[:, lanes]
        v_turned[g] = jnp.transpose(v_all[:, cols(g * DH, DH)])

    @pl.when(zhi == 0)
    def _():
        pl.semaphore_wait(barrier, 1)

    @pl.loop(0, CHUNKS)
    def _(s):
        for k in (1, 3, 2):
            send_y_q(s, k).wait_recv()
        z_q[s, zhi] = pick(host_y, [y_q[s, at] for at in range(NY)])
        send_z_q(s).start()
        pl.when(s + AHEAD < CHUNKS)(lambda: turn_q(s + AHEAD))
        new_tokens(s)

    valid = ctx_ref[0] - seq * context

    def attend(s, half):
        queries = jnp.concatenate([q_full[s, half, h] for h in range(NY)], axis=0)
        keep = lax.broadcasted_iota(jnp.int32, (context, LANES), 0) < valid
        top, total, weights = weigh(k_all[:, cols(s * DH, DH)], queries, keep)
        summed = jnp.dot(v_turned[s], weights, preferred_element_type=jnp.float32)
        new = (new_stats[s, half, 0:1], new_stats[s, half, 1:2], new_sum[s, half])
        return merge([(top, total, summed), new])

    def gather_q(s):
        send_z_q(s).wait_recv()
        q_full[s, core, y] = pick(host_z, [z_q[s, at] for at in range(2)])
        for k in (2, 1, 3):
            send_y_qall(s, k).start()

    def compute_near(s):
        for k in (1, 3, 2):
            send_y_qall(s, k).wait_recv()
        send_core_qall(s).start()
        top, total, summed = attend(s, core)
        o_src[s, 0:DH] = summed
        o_src[s, DH : DH + 1] = top
        o_src[s, DH + 1 : DH + 2] = total
        send_core_o(s).start()

    def compute_far(s):
        send_core_qall(s).wait_recv()
        part = attend(s, other)
        send_core_o(s).wait_recv()
        beside_it = (o_core[s, DH : DH + 1], o_core[s, DH + 1 : DH + 2], o_core[s, 0:DH])
        top, total, summed = merge([part, beside_it])
        packed = pack_stats(top, total)
        for piece in range(NY):
            block = piece // 2
            lanes = slice(block * BLOCK, (block + 1) * BLOCK)
            deep = summed[piece % 2 * DEPTH : (piece % 2 + 1) * DEPTH, lanes]
            y_osrc[s, piece, 0:DEPTH] = deep.astype(jnp.bfloat16)
            y_osrc[s, piece, DEPTH : DEPTH + 16] = packed[:, lanes]
            kept[s, piece, 0:DEPTH] = deep
            kept[s, piece, DEPTH : DEPTH + 1] = top[:, lanes]
            kept[s, piece, DEPTH + 1 : DEPTH + 2] = total[:, lanes]
        for k in (2, 1, 3):
            send_y_o(s, k).start()

    def arrived(ref, *at):
        top, total = unpack_stats(ref[(*at, slice(DEPTH, DEPTH + 16))])
        return top, total, ref[(*at, slice(0, DEPTH))].astype(jnp.float32)

    def sum_y(s):
        for k in (1, 3, 2):
            send_y_o(s, k).wait_recv()
        own = (kept[s, y, DEPTH : DEPTH + 1], kept[s, y, DEPTH + 1 : DEPTH + 2], kept[s, y, 0:DEPTH])
        top, total, summed = merge([own] + [arrived(y_o, s, y_of(k)) for k in (1, 2, 3)])
        z_osrc[s, 0:DEPTH] = summed.astype(jnp.bfloat16)
        z_osrc[s, DEPTH : DEPTH + 16] = pack_stats(top, total)
        send_z_o(s).start()
        half_o[s, 0:DEPTH] = summed
        half_o[s, DEPTH : DEPTH + 1] = top
        half_o[s, DEPTH + 1 : DEPTH + 2] = total

    def sent(single, along_y, s):
        for copy in single:
            copy(s).wait_send()
        for copy in along_y:
            for k in (1, 2, 3):
                copy(s, k).wait_send()

    def finish(s):
        sent((send_core_q, send_z_q, send_core_qall, send_core_o), (send_y_q, send_y_qall, send_y_o), s)
        send_z_o(s).wait_recv()
        own = (half_o[s, DEPTH : DEPTH + 1], half_o[s, DEPTH + 1 : DEPTH + 2], half_o[s, 0:DEPTH])
        _, total, summed = merge([own, arrived(z_o, s)])
        o_pieces[s, other, y] = (summed / total).astype(jnp.bfloat16)
        for k in (2, 1, 3):
            send_y_oall(s, k).start()

    def lay_out(s, half):
        for block in range(2):
            turned = jnp.transpose(
                jnp.concatenate([o_pieces[s, half, 2 * block + e].astype(jnp.float32) for e in range(2)], axis=0)
            ).astype(jnp.bfloat16)
            for h in range(2):
                start = s * CHUNK_COLS + half * HALF_COLS + (2 * block + h) * DH
                o_ref[:, cols(start, DH)] = turned[h * ROWS : (h + 1) * ROWS]

    def gather_o(s):
        for k in (1, 3, 2):
            send_y_oall(s, k).wait_recv()
        send_core_oall(s).start()
        lay_out(s, other)

    def write_o(s):
        send_core_oall(s).wait_recv()
        lay_out(s, core)
        sent((send_z_o, send_core_oall), (send_y_oall,), s)

    @pl.loop(0, CHUNKS + AT_WRITE)
    def _(t):
        for at, stage in (
            (0, gather_q),
            (AT_NEAR, compute_near),
            (AT_FAR, compute_far),
            (AT_SUM, sum_y),
            (AT_FINISH, finish),
            (AT_GATHER, gather_o),
            (AT_WRITE, write_o),
        ):
            pl.when((t >= at) & (t < at + CHUNKS))(functools.partial(stage, t - at))


def attention(query_block, keys, values, ctx_len, host):
    context, width = keys.shape
    bf16, f32 = jnp.bfloat16, jnp.float32
    vmem = pltpu.VMEM
    return pl.pallas_call(
        kernel,
        out_shape=jax.ShapeDtypeStruct((ROWS, HQ * DH), bf16),
        in_specs=[pl.BlockSpec(memory_space=pltpu.SMEM)] * 2 + [pl.BlockSpec(memory_space=pl.ANY)] * 3,
        out_specs=pl.BlockSpec(memory_space=pltpu.VMEM),
        scratch_shapes=[
            vmem(query_block.shape, bf16),
            vmem((context, width), bf16),
            vmem((context, width), bf16),
            vmem((HK, DH, context), bf16),
            vmem((CHUNKS, 2, ROWS, HALF_COLS), bf16),
            vmem((CHUNKS, NY, ROWS, DH), bf16),
            vmem((CHUNKS, NY, ROWS, DH), bf16),
            vmem((CHUNKS, 2, ROWS, DH), bf16),
            vmem((CHUNKS, 2, NY, ROWS, DH), bf16),
            vmem((HK, 2, DH, LANES), f32),
            vmem((HK, 2, 8, LANES), f32),
            vmem((CHUNKS, DH + 8, LANES), f32),
            vmem((CHUNKS, DH + 8, LANES), f32),
            vmem((CHUNKS, NY, DEPTH + 8, BLOCK), f32),
            vmem((CHUNKS, NY, DEPTH + 16, BLOCK), bf16),
            vmem((CHUNKS, NY, DEPTH + 16, BLOCK), bf16),
            vmem((CHUNKS, DEPTH + 8, BLOCK), f32),
            vmem((CHUNKS, DEPTH + 16, BLOCK), bf16),
            vmem((CHUNKS, DEPTH + 16, BLOCK), bf16),
            vmem((CHUNKS, 2, NY, DEPTH, BLOCK), bf16),
            pltpu.SemaphoreType.DMA((4 + CHUNKS,)),
            pltpu.SemaphoreType.DMA((STAGES, CHUNKS)),
            pltpu.SemaphoreType.DMA((STAGES, CHUNKS)),
        ],
        compiler_params=pltpu.CompilerParams(
            collective_id=0, has_side_effects=True, vmem_limit_bytes=52 * 1024 * 1024
        ),
        name="context_attention",
    )(ctx_len, host, query_block, keys, values)


def local(query_block, k_cache, v_cache, ctx_len, host):
    result = attention(query_block[0, 0], k_cache[0], v_cache[0], ctx_len, host)
    result = jnp.where(lax.axis_index("seq") == host[0], result, jnp.zeros((), jnp.bfloat16))
    return result[None, None]


def solution(mesh):
    return jax.shard_map(
        local,
        mesh=mesh,
        in_specs=(
            P("req", "seq", None, None),
            P("req", "seq", None),
            P("req", "seq", None),
            P("req"),
            P("req"),
        ),
        out_specs=P("req", "seq", None, None),
        check_vma=False,
    )
```

```python
import functools
import math

import jax
import jax.numpy as jnp
from jax import lax
from jax.experimental import pallas as pl
from jax.experimental.pallas import tpu as pltpu
from jax.sharding import PartitionSpec as P

HQ = 64
HK = 8
DH = 128
ROWS = 64
NY = 4
CHUNKS = 8
HALF_COLS = HQ // HK * DH // 2
CHUNK_COLS = 2 * HALF_COLS
LANES = 256
BLOCK = 128
DEPTH = DH // 2
SCALE2 = math.log2(math.e) / math.sqrt(DH)
NEG = -1e30
FLOOR = -1e20
ABSENT = -2e20

CORE_Q, Y_Q, Z_Q, Y_QALL, CORE_QALL, CORE_O, Y_O, Z_O, Y_OALL, CORE_OALL = 0, 1, 4, 5, 8, 9, 10, 13, 14, 17
STAGES = 18
AHEAD = 4

AT_NEAR, AT_FAR, AT_SUM, AT_FINISH, AT_GATHER, AT_WRITE = 4, 5, 8, 19, 25, 27


def three_parts(x):
    high = x.astype(jnp.bfloat16).astype(jnp.float32)
    rest = x - high
    mid = rest.astype(jnp.bfloat16).astype(jnp.float32)
    low = (rest - mid).astype(jnp.bfloat16).astype(jnp.float32)
    return high, mid, low


def pack_stats(top, total):
    width = top.shape[1]
    row = lax.broadcasted_iota(jnp.int32, (16, width), 0)
    out = jnp.zeros((16, width), jnp.float32)
    for at, part in enumerate(three_parts(top) + three_parts(total)):
        out = jnp.where(row == at, part, out)
    return out.astype(jnp.bfloat16)


def unpack_stats(packed):
    s = packed.astype(jnp.float32)
    return s[0:1] + s[1:2] + s[2:3], s[3:4] + s[4:5] + s[5:6]


def merge(parts):
    top = functools.reduce(jnp.maximum, [p[0] for p in parts])
    factors = [jnp.exp2((p[0] - top) * SCALE2) for p in parts]
    total = functools.reduce(jnp.add, [p[1] * f for p, f in zip(parts, factors)])
    summed = functools.reduce(jnp.add, [p[2] * f for p, f in zip(parts, factors)])
    return top, total, summed


def weigh(keys, queries, keep):
    scores = lax.dot_general(keys, queries, (((1,), (1,)), ((), ())), preferred_element_type=jnp.float32)
    scores = jnp.where(keep, scores, NEG)
    top = jnp.maximum(jnp.max(scores, axis=0, keepdims=True), FLOOR)
    weights = jnp.exp2((scores - top) * SCALE2)
    return top, jnp.sum(weights, axis=0, keepdims=True), weights.astype(jnp.bfloat16)


def kernel(
    ctx_ref, host_ref, q_hbm, k_hbm, v_hbm, o_ref,
    q_all, k_all, v_all, v_turned, core_q, y_src, y_q, z_q, q_full,
    new_sum, new_stats, o_src, o_core, kept, y_osrc, y_o, half_o, z_osrc, z_o, o_pieces,
    local_sem, send_sem, recv_sem,
):
    context = k_hbm.shape[0]
    seq = lax.axis_index("seq")
    core = lax.rem(seq, 2)
    zhi = lax.rem(lax.div(seq, 2), 2)
    y = lax.div(seq, 4)
    other = 1 - core
    sibling = seq + 1 - 2 * core
    across = seq + 2 - 4 * zhi

    host = host_ref[0]
    host_core = lax.rem(host, 2)
    host_z = lax.rem(lax.div(host, 2), 2)
    host_y = lax.div(host, 4)

    def pick(index, values):
        out = values[0]
        for at in range(1, len(values)):
            out = lax.select(index == at, values[at], out)
        return out

    def cols(start, size):
        return pl.ds(pl.multiple_of(start, 128), size)

    def y_of(k):
        return lax.rem(y + k, NY)

    def beside(k):
        return lax.rem(seq + 4 * k, 16)

    def remote(src, dst, stage, s, to):
        return pltpu.make_async_remote_copy(
            src_ref=src,
            dst_ref=dst,
            send_sem=send_sem.at[stage, s],
            recv_sem=recv_sem.at[stage, s],
            device_id={"seq": to},
            device_id_type=pl.DeviceIdType.MESH,
        )

    def send_core_q(s):
        return remote(
            q_all.at[:, cols(s * CHUNK_COLS + other * HALF_COLS, HALF_COLS)], core_q.at[s], CORE_Q, s, sibling
        )

    def send_y_q(s, k):
        return remote(y_src.at[s, y_of(k)], y_q.at[s, y], Y_Q + k - 1, s, beside(k))

    def send_z_q(s):
        return remote(z_q.at[s, zhi], z_q.at[s, zhi], Z_Q, s, across)

    def send_y_qall(s, k):
        piece = q_full.at[s, core, y]
        return remote(piece, piece, Y_QALL + k - 1, s, beside(k))

    def send_core_qall(s):
        return remote(q_full.at[s, core], q_full.at[s, core], CORE_QALL, s, sibling)

    def send_core_o(s):
        return remote(o_src.at[s], o_core.at[s], CORE_O, s, sibling)

    def send_y_o(s, k):
        return remote(y_osrc.at[s, y_of(k)], y_o.at[s, y], Y_O + k - 1, s, beside(k))

    def send_z_o(s):
        return remote(z_osrc.at[s], z_o.at[s], Z_O, s, across)

    def send_y_oall(s, k):
        piece = o_pieces.at[s, other, y]
        return remote(piece, piece, Y_OALL + k - 1, s, beside(k))

    def send_core_oall(s):
        return remote(o_pieces.at[s, other], o_pieces.at[s, other], CORE_OALL, s, sibling)

    loads = [
        pltpu.make_async_copy(src, dst, local_sem.at[at])
        for at, (src, dst) in enumerate(((q_hbm, q_all), (k_hbm, k_all), (v_hbm, v_all)))
    ]
    barrier = pltpu.get_barrier_semaphore()

    def greet(to):
        pl.semaphore_signal(barrier, inc=1, device_id={"seq": to}, device_id_type=pl.DeviceIdType.MESH)

    for to in (beside(2), beside(1), beside(3), sibling):
        greet(to)
    for copy in loads:
        copy.start()

    @pl.when(zhi == 0)
    def _():
        pl.semaphore_wait(barrier, 4)
        greet(across)

    @pl.when(zhi == 1)
    def _():
        pl.semaphore_wait(barrier, 5)
        greet(across)

    loads[0].wait()

    @pl.loop(0, CHUNKS)
    def _(s):
        send_core_q(s).start()

    def turn_q(s):
        send_core_q(s).wait_recv()
        for at in range(NY):
            own = q_all[:, cols(s * CHUNK_COLS + core * HALF_COLS + at * DH, DH)]
            y_src[s, at] = lax.select(host_core == core, own, core_q[s, :, at * DH : (at + 1) * DH])
        for k in (2, 1, 3):
            send_y_q(s, k).start()
        y_q[s, y] = y_src[s, y]

    pl.loop(0, AHEAD)(turn_q)

    for copy in loads[1:]:
        copy.wait()
    is_host = jnp.broadcast_to(host, (1, 2 * LANES)) == jnp.broadcast_to(seq, (1, 2 * LANES))
    causal = lax.broadcasted_iota(jnp.int32, (ROWS, 2 * LANES), 0) <= lax.rem(
        lax.broadcasted_iota(jnp.int32, (ROWS, 2 * LANES), 1), ROWS
    )

    def new_tokens(g):
        queries = jnp.concatenate(
            [q_all[:, cols(g * CHUNK_COLS + h * DH, DH)] for h in range(HQ // HK)], axis=0
        )
        new_keys = q_all[:, cols(HQ * DH + g * DH, DH)]
        new_values = q_all[:, cols((HQ + HK) * DH + g * DH, DH)]
        top, total, weights = weigh(new_keys, queries, causal)
        summed = lax.dot_general(
            new_values, weights, (((0,), (0,)), ((), ())), preferred_element_type=jnp.float32
        )
        top = jnp.where(is_host, top, ABSENT)
        for half in range(2):
            lanes = slice(half * LANES, (half + 1) * LANES)
            new_sum[g, half] = summed[:, lanes]
            new_stats[g, half, 0:1] = top[:, lanes]
            new_stats[g, half, 1:2] = total[:, lanes]
        v_turned[g] = jnp.transpose(v_all[:, cols(g * DH, DH)])

    @pl.when(zhi == 0)
    def _():
        pl.semaphore_wait(barrier, 1)

    @pl.loop(0, CHUNKS)
    def _(s):
        for k in (1, 3, 2):
            send_y_q(s, k).wait_recv()
        z_q[s, zhi] = pick(host_y, [y_q[s, at] for at in range(NY)])
        send_z_q(s).start()
        pl.when(s + AHEAD < CHUNKS)(lambda: turn_q(s + AHEAD))

    valid = ctx_ref[0] - seq * context

    def attend(s, half):
        queries = jnp.concatenate([q_full[s, half, h] for h in range(NY)], axis=0)
        keep = lax.broadcasted_iota(jnp.int32, (context, LANES), 0) < valid
        top, total, weights = weigh(k_all[:, cols(s * DH, DH)], queries, keep)
        summed = jnp.dot(v_turned[s], weights, preferred_element_type=jnp.float32)
        new = (new_stats[s, half, 0:1], new_stats[s, half, 1:2], new_sum[s, half])
        return merge([(top, total, summed), new])

    def gather_q(s):
        send_z_q(s).wait_recv()
        q_full[s, core, y] = pick(host_z, [z_q[s, at] for at in range(2)])
        for k in (2, 1, 3):
            send_y_qall(s, k).start()

        @pl.when(s < HK // 2)
        def _():
            new_tokens(2 * s)
            new_tokens(2 * s + 1)

    def compute_near(s):
        for k in (1, 3, 2):
            send_y_qall(s, k).wait_recv()
        send_core_qall(s).start()
        top, total, summed = attend(s, core)
        o_src[s, 0:DH] = summed
        o_src[s, DH : DH + 1] = top
        o_src[s, DH + 1 : DH + 2] = total
        send_core_o(s).start()

    def compute_far(s):
        send_core_qall(s).wait_recv()
        part = attend(s, other)
        send_core_o(s).wait_recv()
        beside_it = (o_core[s, DH : DH + 1], o_core[s, DH + 1 : DH + 2], o_core[s, 0:DH])
        top, total, summed = merge([part, beside_it])
        packed = pack_stats(top, total)
        for piece in range(NY):
            block = piece // 2
            lanes = slice(block * BLOCK, (block + 1) * BLOCK)
            deep = summed[piece % 2 * DEPTH : (piece % 2 + 1) * DEPTH, lanes]
            y_osrc[s, piece, 0:DEPTH] = deep.astype(jnp.bfloat16)
            y_osrc[s, piece, DEPTH : DEPTH + 16] = packed[:, lanes]
            kept[s, piece, 0:DEPTH] = deep
            kept[s, piece, DEPTH : DEPTH + 1] = top[:, lanes]
            kept[s, piece, DEPTH + 1 : DEPTH + 2] = total[:, lanes]
        for k in (2, 1, 3):
            send_y_o(s, k).start()

    def arrived(ref, *at):
        top, total = unpack_stats(ref[(*at, slice(DEPTH, DEPTH + 16))])
        return top, total, ref[(*at, slice(0, DEPTH))].astype(jnp.float32)

    def sum_y(s):
        for k in (1, 3, 2):
            send_y_o(s, k).wait_recv()
        own = (kept[s, y, DEPTH : DEPTH + 1], kept[s, y, DEPTH + 1 : DEPTH + 2], kept[s, y, 0:DEPTH])
        top, total, summed = merge([own] + [arrived(y_o, s, y_of(k)) for k in (1, 2, 3)])
        z_osrc[s, 0:DEPTH] = summed.astype(jnp.bfloat16)
        z_osrc[s, DEPTH : DEPTH + 16] = pack_stats(top, total)
        send_z_o(s).start()
        half_o[s, 0:DEPTH] = summed
        half_o[s, DEPTH : DEPTH + 1] = top
        half_o[s, DEPTH + 1 : DEPTH + 2] = total

    def sent(single, along_y, s):
        for copy in single:
            copy(s).wait_send()
        for copy in along_y:
            for k in (1, 2, 3):
                copy(s, k).wait_send()

    def finish(s):
        sent((send_core_q, send_z_q, send_core_qall, send_core_o), (send_y_q, send_y_qall, send_y_o), s)
        send_z_o(s).wait_recv()
        own = (half_o[s, DEPTH : DEPTH + 1], half_o[s, DEPTH + 1 : DEPTH + 2], half_o[s, 0:DEPTH])
        _, total, summed = merge([own, arrived(z_o, s)])
        o_pieces[s, other, y] = (summed / total).astype(jnp.bfloat16)
        for k in (2, 1, 3):
            send_y_oall(s, k).start()

    def lay_out(s, half):
        for block in range(2):
            turned = jnp.transpose(
                jnp.concatenate([o_pieces[s, half, 2 * block + e].astype(jnp.float32) for e in range(2)], axis=0)
            ).astype(jnp.bfloat16)
            for h in range(2):
                start = s * CHUNK_COLS + half * HALF_COLS + (2 * block + h) * DH
                o_ref[:, cols(start, DH)] = turned[h * ROWS : (h + 1) * ROWS]

    def gather_o(s):
        for k in (1, 3, 2):
            send_y_oall(s, k).wait_recv()
        send_core_oall(s).start()
        lay_out(s, other)

    def write_o(s):
        send_core_oall(s).wait_recv()
        lay_out(s, core)
        sent((send_z_o, send_core_oall), (send_y_oall,), s)

    @pl.loop(0, CHUNKS + AT_WRITE)
    def _(t):
        for at, stage in (
            (0, gather_q),
            (AT_NEAR, compute_near),
            (AT_FAR, compute_far),
            (AT_SUM, sum_y),
            (AT_FINISH, finish),
            (AT_GATHER, gather_o),
            (AT_WRITE, write_o),
        ):
            pl.when((t >= at) & (t < at + CHUNKS))(functools.partial(stage, t - at))


def attention(query_block, keys, values, ctx_len, host):
    context, width = keys.shape
    bf16, f32 = jnp.bfloat16, jnp.float32
    vmem = pltpu.VMEM
    return pl.pallas_call(
        kernel,
        out_shape=jax.ShapeDtypeStruct((ROWS, HQ * DH), bf16),
        in_specs=[pl.BlockSpec(memory_space=pltpu.SMEM)] * 2 + [pl.BlockSpec(memory_space=pl.ANY)] * 3,
        out_specs=pl.BlockSpec(memory_space=pltpu.VMEM),
        scratch_shapes=[
            vmem(query_block.shape, bf16),
            vmem((context, width), bf16),
            vmem((context, width), bf16),
            vmem((HK, DH, context), bf16),
            vmem((CHUNKS, ROWS, HALF_COLS), bf16),
            vmem((CHUNKS, NY, ROWS, DH), bf16),
            vmem((CHUNKS, NY, ROWS, DH), bf16),
            vmem((CHUNKS, 2, ROWS, DH), bf16),
            vmem((CHUNKS, 2, NY, ROWS, DH), bf16),
            vmem((HK, 2, DH, LANES), f32),
            vmem((HK, 2, 8, LANES), f32),
            vmem((CHUNKS, DH + 8, LANES), f32),
            vmem((CHUNKS, DH + 8, LANES), f32),
            vmem((CHUNKS, NY, DEPTH + 8, BLOCK), f32),
            vmem((CHUNKS, NY, DEPTH + 16, BLOCK), bf16),
            vmem((CHUNKS, NY, DEPTH + 16, BLOCK), bf16),
            vmem((CHUNKS, DEPTH + 8, BLOCK), f32),
            vmem((CHUNKS, DEPTH + 16, BLOCK), bf16),
            vmem((CHUNKS, DEPTH + 16, BLOCK), bf16),
            vmem((CHUNKS, 2, NY, DEPTH, BLOCK), bf16),
            pltpu.SemaphoreType.DMA((3,)),
            pltpu.SemaphoreType.DMA((STAGES, CHUNKS)),
            pltpu.SemaphoreType.DMA((STAGES, CHUNKS)),
        ],
        compiler_params=pltpu.CompilerParams(
            collective_id=0, has_side_effects=True, vmem_limit_bytes=52 * 1024 * 1024
        ),
        name="context_attention",
    )(ctx_len, host, query_block, keys, values)


def local(query_block, k_cache, v_cache, ctx_len, host):
    result = attention(query_block[0, 0], k_cache[0], v_cache[0], ctx_len, host)
    result = jnp.where(lax.axis_index("seq") == host[0], result, jnp.zeros((), jnp.bfloat16))
    return result[None, None]


def solution(mesh):
    return jax.shard_map(
        local,
        mesh=mesh,
        in_specs=(
            P("req", "seq", None, None),
            P("req", "seq", None),
            P("req", "seq", None),
            P("req"),
            P("req"),
        ),
        out_specs=P("req", "seq", None, None),
        check_vma=False,
    )
```

```python
import functools
import math

import jax
import jax.numpy as jnp
from jax import lax
from jax.experimental import pallas as pl
from jax.experimental.pallas import tpu as pltpu
from jax.sharding import PartitionSpec as P

HQ = 64
HK = 8
DH = 128
ROWS = 64
NY = 4
CHUNKS = 8
HALF_COLS = HQ // HK * DH // 2
CHUNK_COLS = 2 * HALF_COLS
LANES = 256
BLOCK = 128
DEPTH = DH // 2
SCALE2 = math.log2(math.e) / math.sqrt(DH)
NEG = -1e30
FLOOR = -1e20
ABSENT = -2e20

CORE_Q, Y_Q, Z_Q, Y_QALL, CORE_QALL, CORE_O, Y_O, Z_O, Y_OALL, CORE_OALL = 0, 1, 4, 5, 8, 9, 10, 13, 14, 17
STAGES = 18
AHEAD = 5

AT_NEAR, AT_FAR, AT_SUM, AT_FINISH, AT_GATHER, AT_WRITE = 4, 5, 8, 18, 24, 26


def three_parts(x):
    high = x.astype(jnp.bfloat16).astype(jnp.float32)
    rest = x - high
    mid = rest.astype(jnp.bfloat16).astype(jnp.float32)
    low = (rest - mid).astype(jnp.bfloat16).astype(jnp.float32)
    return high, mid, low


def pack_stats(top, total):
    width = top.shape[1]
    row = lax.broadcasted_iota(jnp.int32, (16, width), 0)
    out = jnp.zeros((16, width), jnp.float32)
    for at, part in enumerate(three_parts(top) + three_parts(total)):
        out = jnp.where(row == at, part, out)
    return out.astype(jnp.bfloat16)


def unpack_stats(packed):
    s = packed.astype(jnp.float32)
    return s[0:1] + s[1:2] + s[2:3], s[3:4] + s[4:5] + s[5:6]


def merge(parts):
    top = functools.reduce(jnp.maximum, [p[0] for p in parts])
    factors = [jnp.exp2((p[0] - top) * SCALE2) for p in parts]
    total = functools.reduce(jnp.add, [p[1] * f for p, f in zip(parts, factors)])
    summed = functools.reduce(jnp.add, [p[2] * f for p, f in zip(parts, factors)])
    return top, total, summed


def weigh(keys, queries, keep):
    scores = lax.dot_general(keys, queries, (((1,), (1,)), ((), ())), preferred_element_type=jnp.float32)
    scores = jnp.where(keep, scores, NEG)
    top = jnp.maximum(jnp.max(scores, axis=0, keepdims=True), FLOOR)
    weights = jnp.exp2((scores - top) * SCALE2)
    return top, jnp.sum(weights, axis=0, keepdims=True), weights.astype(jnp.bfloat16)


def kernel(
    ctx_ref, host_ref, q_hbm, k_hbm, v_hbm, o_ref,
    q_all, k_all, v_all, v_turned, core_q, y_src, y_q, z_q, q_full,
    new_sum, new_stats, o_src, o_core, kept, y_osrc, y_o, half_o, z_osrc, z_o, o_pieces,
    local_sem, send_sem, recv_sem,
):
    context = k_hbm.shape[0]
    seq = lax.axis_index("seq")
    core = lax.rem(seq, 2)
    zhi = lax.rem(lax.div(seq, 2), 2)
    y = lax.div(seq, 4)
    other = 1 - core
    sibling = seq + 1 - 2 * core
    across = seq + 2 - 4 * zhi

    host = host_ref[0]
    host_core = lax.rem(host, 2)
    host_z = lax.rem(lax.div(host, 2), 2)
    host_y = lax.div(host, 4)

    def pick(index, values):
        out = values[0]
        for at in range(1, len(values)):
            out = lax.select(index == at, values[at], out)
        return out

    def cols(start, size):
        return pl.ds(pl.multiple_of(start, 128), size)

    def y_of(k):
        return lax.rem(y + k, NY)

    def beside(k):
        return lax.rem(seq + 4 * k, 16)

    def remote(src, dst, stage, s, to):
        return pltpu.make_async_remote_copy(
            src_ref=src,
            dst_ref=dst,
            send_sem=send_sem.at[stage, s],
            recv_sem=recv_sem.at[stage, s],
            device_id={"seq": to},
            device_id_type=pl.DeviceIdType.MESH,
        )

    def send_core_q(s):
        return remote(
            q_hbm.at[:, cols(s * CHUNK_COLS + other * HALF_COLS, HALF_COLS)], core_q.at[s, core], CORE_Q, s, sibling
        )

    def send_y_q(s, k):
        return remote(y_src.at[s, y_of(k)], y_q.at[s, y], Y_Q + k - 1, s, beside(k))

    def send_z_q(s):
        return remote(z_q.at[s, zhi], z_q.at[s, zhi], Z_Q, s, across)

    def send_y_qall(s, k):
        piece = q_full.at[s, core, y]
        return remote(piece, piece, Y_QALL + k - 1, s, beside(k))

    def send_core_qall(s):
        return remote(q_full.at[s, core], q_full.at[s, core], CORE_QALL, s, sibling)

    def send_core_o(s):
        return remote(o_src.at[s], o_core.at[s], CORE_O, s, sibling)

    def send_y_o(s, k):
        return remote(y_osrc.at[s, y_of(k)], y_o.at[s, y], Y_O + k - 1, s, beside(k))

    def send_z_o(s):
        return remote(z_osrc.at[s], z_o.at[s], Z_O, s, across)

    def send_y_oall(s, k):
        piece = o_pieces.at[s, other, y]
        return remote(piece, piece, Y_OALL + k - 1, s, beside(k))

    def send_core_oall(s):
        return remote(o_pieces.at[s, other], o_pieces.at[s, other], CORE_OALL, s, sibling)

    def own_q(s):
        return pltpu.make_async_copy(
            q_hbm.at[:, cols(s * CHUNK_COLS + core * HALF_COLS, HALF_COLS)], core_q.at[s, core], local_sem.at[4 + s]
        )

    loads = [
        pltpu.make_async_copy(src, dst, local_sem.at[at])
        for at, (src, dst) in enumerate(((q_hbm, q_all), (k_hbm, k_all), (v_hbm, v_all)))
    ]
    barrier = pltpu.get_barrier_semaphore()

    def greet(to):
        pl.semaphore_signal(barrier, inc=1, device_id={"seq": to}, device_id_type=pl.DeviceIdType.MESH)

    for to in (beside(2), beside(1), beside(3), sibling):
        greet(to)
    for s in range(CHUNKS):
        own_q(s).start()
    for copy in loads:
        copy.start()

    @pl.when(zhi == 0)
    def _():
        pl.semaphore_wait(barrier, 4)
        greet(across)

    @pl.when(zhi == 1)
    def _():
        pl.semaphore_wait(barrier, 5)
        greet(across)

    @pl.loop(0, CHUNKS)
    def _(s):
        send_core_q(s).start()

    def turn_q(s):
        own_q(s).wait()
        send_core_q(s).wait_recv()
        for at in range(NY):
            piece = slice(at * DH, (at + 1) * DH)
            y_src[s, at] = pick(host_core, [core_q[s, c, :, piece] for c in range(2)])
        for k in (2, 1, 3):
            send_y_q(s, k).start()
        y_q[s, y] = y_src[s, y]

    pl.loop(0, AHEAD)(turn_q)

    for copy in loads:
        copy.wait()
    is_host = jnp.broadcast_to(host, (1, 2 * LANES)) == jnp.broadcast_to(seq, (1, 2 * LANES))
    causal = lax.broadcasted_iota(jnp.int32, (ROWS, 2 * LANES), 0) <= lax.rem(
        lax.broadcasted_iota(jnp.int32, (ROWS, 2 * LANES), 1), ROWS
    )

    def new_tokens(g):
        queries = jnp.concatenate(
            [q_all[:, cols(g * CHUNK_COLS + h * DH, DH)] for h in range(HQ // HK)], axis=0
        )
        new_keys = q_all[:, cols(HQ * DH + g * DH, DH)]
        new_values = q_all[:, cols((HQ + HK) * DH + g * DH, DH)]
        top, total, weights = weigh(new_keys, queries, causal)
        summed = lax.dot_general(
            new_values, weights, (((0,), (0,)), ((), ())), preferred_element_type=jnp.float32
        )
        top = jnp.where(is_host, top, ABSENT)
        for half in range(2):
            lanes = slice(half * LANES, (half + 1) * LANES)
            new_sum[g, half] = summed[:, lanes]
            new_stats[g, half, 0:1] = top[:, lanes]
            new_stats[g, half, 1:2] = total[:, lanes]
        v_turned[g] = jnp.transpose(v_all[:, cols(g * DH, DH)])

    @pl.when(zhi == 0)
    def _():
        pl.semaphore_wait(barrier, 1)

    @pl.loop(0, CHUNKS)
    def _(s):
        for k in (1, 3, 2):
            send_y_q(s, k).wait_recv()
        z_q[s, zhi] = pick(host_y, [y_q[s, at] for at in range(NY)])
        send_z_q(s).start()
        pl.when(s + AHEAD < CHUNKS)(lambda: turn_q(s + AHEAD))
        new_tokens(s)

    valid = ctx_ref[0] - seq * context

    def attend(s, half):
        queries = jnp.concatenate([q_full[s, half, h] for h in range(NY)], axis=0)
        keep = lax.broadcasted_iota(jnp.int32, (context, LANES), 0) < valid
        top, total, weights = weigh(k_all[:, cols(s * DH, DH)], queries, keep)
        summed = jnp.dot(v_turned[s], weights, preferred_element_type=jnp.float32)
        new = (new_stats[s, half, 0:1], new_stats[s, half, 1:2], new_sum[s, half])
        return merge([(top, total, summed), new])

    def gather_q(s):
        send_z_q(s).wait_recv()
        q_full[s, core, y] = pick(host_z, [z_q[s, at] for at in range(2)])
        for k in (2, 1, 3):
            send_y_qall(s, k).start()

    def compute_near(s):
        for k in (1, 3, 2):
            send_y_qall(s, k).wait_recv()
        send_core_qall(s).start()
        top, total, summed = attend(s, core)
        o_src[s, 0:DH] = summed
        o_src[s, DH : DH + 1] = top
        o_src[s, DH + 1 : DH + 2] = total
        send_core_o(s).start()

    def compute_far(s):
        send_core_qall(s).wait_recv()
        part = attend(s, other)
        send_core_o(s).wait_recv()
        beside_it = (o_core[s, DH : DH + 1], o_core[s, DH + 1 : DH + 2], o_core[s, 0:DH])
        top, total, summed = merge([part, beside_it])
        packed = pack_stats(top, total)
        for piece in range(NY):
            block = piece // 2
            lanes = slice(block * BLOCK, (block + 1) * BLOCK)
            deep = summed[piece % 2 * DEPTH : (piece % 2 + 1) * DEPTH, lanes]
            y_osrc[s, piece, 0:DEPTH] = deep.astype(jnp.bfloat16)
            y_osrc[s, piece, DEPTH : DEPTH + 16] = packed[:, lanes]
        for k in (2, 1, 3):
            send_y_o(s, k).start()
        for piece in range(NY):
            block = piece // 2
            lanes = slice(block * BLOCK, (block + 1) * BLOCK)
            kept[s, piece, 0:DEPTH] = summed[piece % 2 * DEPTH : (piece % 2 + 1) * DEPTH, lanes]
            kept[s, piece, DEPTH : DEPTH + 1] = top[:, lanes]
            kept[s, piece, DEPTH + 1 : DEPTH + 2] = total[:, lanes]

    def arrived(ref, *at):
        top, total = unpack_stats(ref[(*at, slice(DEPTH, DEPTH + 16))])
        return top, total, ref[(*at, slice(0, DEPTH))].astype(jnp.float32)

    def sum_y(s):
        for k in (1, 3, 2):
            send_y_o(s, k).wait_recv()
        own = (kept[s, y, DEPTH : DEPTH + 1], kept[s, y, DEPTH + 1 : DEPTH + 2], kept[s, y, 0:DEPTH])
        top, total, summed = merge([own] + [arrived(y_o, s, y_of(k)) for k in (1, 2, 3)])
        z_osrc[s, 0:DEPTH] = summed.astype(jnp.bfloat16)
        z_osrc[s, DEPTH : DEPTH + 16] = pack_stats(top, total)
        send_z_o(s).start()
        half_o[s, 0:DEPTH] = summed
        half_o[s, DEPTH : DEPTH + 1] = top
        half_o[s, DEPTH + 1 : DEPTH + 2] = total

    def sent(single, along_y, s):
        for copy in single:
            copy(s).wait_send()
        for copy in along_y:
            for k in (1, 2, 3):
                copy(s, k).wait_send()

    def finish(s):
        sent((send_core_q, send_z_q, send_core_qall, send_core_o), (send_y_q, send_y_qall, send_y_o), s)
        send_z_o(s).wait_recv()
        own = (half_o[s, DEPTH : DEPTH + 1], half_o[s, DEPTH + 1 : DEPTH + 2], half_o[s, 0:DEPTH])
        _, total, summed = merge([own, arrived(z_o, s)])
        o_pieces[s, other, y] = (summed / total).astype(jnp.bfloat16)
        for k in (2, 1, 3):
            send_y_oall(s, k).start()

    def lay_out(s, half):
        for block in range(2):
            turned = jnp.transpose(
                jnp.concatenate([o_pieces[s, half, 2 * block + e].astype(jnp.float32) for e in range(2)], axis=0)
            ).astype(jnp.bfloat16)
            for h in range(2):
                start = s * CHUNK_COLS + half * HALF_COLS + (2 * block + h) * DH
                o_ref[:, cols(start, DH)] = turned[h * ROWS : (h + 1) * ROWS]

    def gather_o(s):
        for k in (1, 3, 2):
            send_y_oall(s, k).wait_recv()
        send_core_oall(s).start()
        lay_out(s, other)

    def write_o(s):
        send_core_oall(s).wait_recv()
        lay_out(s, core)
        sent((send_z_o, send_core_oall), (send_y_oall,), s)

    @pl.loop(0, CHUNKS + AT_WRITE)
    def _(t):
        for at, stage in (
            (0, gather_q),
            (AT_NEAR, compute_near),
            (AT_FAR, compute_far),
            (AT_SUM, sum_y),
            (AT_FINISH, finish),
            (AT_GATHER, gather_o),
            (AT_WRITE, write_o),
        ):
            pl.when((t >= at) & (t < at + CHUNKS))(functools.partial(stage, t - at))


def attention(query_block, keys, values, ctx_len, host):
    context, width = keys.shape
    bf16, f32 = jnp.bfloat16, jnp.float32
    vmem = pltpu.VMEM
    return pl.pallas_call(
        kernel,
        out_shape=jax.ShapeDtypeStruct((ROWS, HQ * DH), bf16),
        in_specs=[pl.BlockSpec(memory_space=pltpu.SMEM)] * 2 + [pl.BlockSpec(memory_space=pl.ANY)] * 3,
        out_specs=pl.BlockSpec(memory_space=pltpu.VMEM),
        scratch_shapes=[
            vmem(query_block.shape, bf16),
            vmem((context, width), bf16),
            vmem((context, width), bf16),
            vmem((HK, DH, context), bf16),
            vmem((CHUNKS, 2, ROWS, HALF_COLS), bf16),
            vmem((CHUNKS, NY, ROWS, DH), bf16),
            vmem((CHUNKS, NY, ROWS, DH), bf16),
            vmem((CHUNKS, 2, ROWS, DH), bf16),
            vmem((CHUNKS, 2, NY, ROWS, DH), bf16),
            vmem((HK, 2, DH, LANES), f32),
            vmem((HK, 2, 8, LANES), f32),
            vmem((CHUNKS, DH + 8, LANES), f32),
            vmem((CHUNKS, DH + 8, LANES), f32),
            vmem((CHUNKS, NY, DEPTH + 8, BLOCK), f32),
            vmem((CHUNKS, NY, DEPTH + 16, BLOCK), bf16),
            vmem((CHUNKS, NY, DEPTH + 16, BLOCK), bf16),
            vmem((CHUNKS, DEPTH + 8, BLOCK), f32),
            vmem((CHUNKS, DEPTH + 16, BLOCK), bf16),
            vmem((CHUNKS, DEPTH + 16, BLOCK), bf16),
            vmem((CHUNKS, 2, NY, DEPTH, BLOCK), bf16),
            pltpu.SemaphoreType.DMA((4 + CHUNKS,)),
            pltpu.SemaphoreType.DMA((STAGES, CHUNKS)),
            pltpu.SemaphoreType.DMA((STAGES, CHUNKS)),
        ],
        compiler_params=pltpu.CompilerParams(
            collective_id=0, has_side_effects=True, vmem_limit_bytes=52 * 1024 * 1024
        ),
        name="context_attention",
    )(ctx_len, host, query_block, keys, values)


def local(query_block, k_cache, v_cache, ctx_len, host):
    result = attention(query_block[0, 0], k_cache[0], v_cache[0], ctx_len, host)
    result = jnp.where(lax.axis_index("seq") == host[0], result, jnp.zeros((), jnp.bfloat16))
    return result[None, None]


def solution(mesh):
    return jax.shard_map(
        local,
        mesh=mesh,
        in_specs=(
            P("req", "seq", None, None),
            P("req", "seq", None),
            P("req", "seq", None),
            P("req"),
            P("req"),
        ),
        out_specs=P("req", "seq", None, None),
        check_vma=False,
    )
```
